256 devices in a mesh: dp: 4 (over x), seq: 64 (over z, y, core).
Axes of the slice: x: 4, y: 4, z: 8, core: 2. Of those that a mesh axis runs over, the one named last changes fastest.
Arguments:
- hidden_states: bfloat16 [32768, 4096], P(('dp', 'seq')), may hold values from -32 to 32
- q_grads: bfloat16 [32768, 4096], P(('dp', 'seq')), may hold values from -48 to 48
- doc_units: int32 [4, 3], P('dp'), may hold values from 1 to 48, 64 in all within a row
Outputs:
- doc_ratio: float32 [4, 3], P('dp')
- clipped_grad: float32 [64, 512, 512], P('seq', 'dp')
The draws below stay inside these ranges and needn't reach their ends.
Inputs may be any that keep to these rules, and one draw needn't show every extreme that they name: `doc_units`: each row lists, in order, the lengths of the documents packed into one group's 8192 tokens; a row sums to 64, and each row holds 48 somewhere.
All inputs are finite; a program needn't handle non-finite values.
Results may differ from the reference program's by a relative error of at most 0.00038.
Values may be sent and summed in bfloat16 or wider, within the bound.
No kernel may reach another device: no remote copies, remote signals or barrier semaphores. Data moves between devices by JAX's collectives and lax.ppermute only.
A program may use at most 128 MiB of HBM per device.

```python
import math
import jax
import jax.numpy as jnp
import numpy as np
from jax import lax

D = 4096
UNIT = 128
DOCS = 3
COL_TILES = 8
ROW_TILES = 8
PACK = 8192
MOST_UNITS = 48
TOKENS = 32768
TILE_R = 512
TILE_C = 512
N_DP = 4
N_SEQ = 64


def scale_draw(key, count, low_end, high_end):
    return jnp.exp(jax.random.uniform(key, (count,), jnp.float32, math.log(low_end), math.log(high_end)))


def draw_hidden_states(key, part):
    key = jax.random.fold_in(key, 7)
    subkeys = jax.random.split(key, 4)
    noise_part = jax.random.truncated_normal(subkeys[0], -4.0, 4.0, (TOKENS, D), jnp.float32)
    common = 0.25
    row_scale = scale_draw(subkeys[2], TOKENS, 0.5, 2.0)
    col_scale = scale_draw(subkeys[3], D, 0.3, 3.0)
    shared = jax.random.truncated_normal(subkeys[1], -4.0, 4.0, (D,), jnp.float32)
    values = (noise_part + common * shared[None, :]) * row_scale[:, None] * col_scale[None, :]
    return values.astype(jnp.bfloat16)


def draw_q_grads(key, part):
    key = jax.random.fold_in(key, 13)
    subkeys = jax.random.split(key, 3)
    noise_part = jax.random.truncated_normal(subkeys[0], -4.0, 4.0, (TOKENS, D), jnp.float32)
    common = 0.25
    shared = jax.random.truncated_normal(subkeys[1], -4.0, 4.0, (D,), jnp.float32)
    row_scale = scale_draw(subkeys[2], TOKENS, 0.3, 3.0)
    positions = (jnp.arange(TOKENS, dtype=jnp.int32) % PACK).astype(jnp.float32)
    rising = 1.0 + 2.0 * positions / PACK
    values = (noise_part + common * shared[None, :]) * (row_scale * rising)[:, None]
    return values.astype(jnp.bfloat16)


def profile(amount, total, limit, slope):
    weights = [(1 << 20) // math.isqrt(standing ** slope) + 1 for standing in range(2, amount + 1)]
    rest, given = total - limit - (amount - 1), [1] * (amount - 1)
    while rest > 0:
        free = [i for i in range(amount - 1) if given[i] < limit]
        mass, left = sum([weights[i] for i in free]), rest
        for i in free:
            more = min(limit - given[i], max(1, left * weights[i] // mass), rest)
            given[i] = given[i] + more
            rest = rest - more
    return np.array([limit] + given)


def ragged_sizes(rng, amount, total, limit, skew):
    if amount == 2:
        one = jax.random.randint(rng, (), max(1, total - limit), min(limit, total - 1) + 1)
        return jnp.stack([one, total - one])
    tallies = jnp.asarray(profile(amount, total, limit, skew), jnp.int32)
    couples = (amount - 1) // 2
    giver, taker = tallies[1:1 + 2 * couples:2], tallies[2:2 + 2 * couples:2]
    slack = jnp.minimum(giver - 1, limit - taker)
    shifted = jax.random.randint(jax.random.fold_in(rng, 1), (couples,), 0, 1 << 20) % (slack + 1)
    tallies = tallies.at[1:1 + 2 * couples:2].set(giver - shifted).at[2:2 + 2 * couples:2].set(taker + shifted)
    return tallies[jax.random.permutation(jax.random.fold_in(rng, 2), amount)]


def setup_inputs(seed: int = 0) -> dict:
    arg_keys = jax.random.split(jax.random.key(seed), 4)
    return {
        "hidden_states": draw_hidden_states(jax.random.fold_in(arg_keys[3], 71), 0),
        "q_grads": draw_q_grads(jax.random.fold_in(arg_keys[3], 71), 0),
        "doc_units": jax.vmap(lambda own: ragged_sizes(own, DOCS, PACK // UNIT, MOST_UNITS, 1))(jax.random.split(arg_keys[2], N_DP)).reshape((N_DP, DOCS)).astype(jnp.int32),
    }


def reference(hidden_states, q_grads, doc_units):
    unit_count = PACK // UNIT
    token_acts = hidden_states.reshape(N_DP, PACK, D)
    token_grads = q_grads.reshape(N_DP, PACK, D)
    lengths = (doc_units * UNIT).astype(jnp.int32)
    doc_ends = jnp.cumsum(lengths, axis=1).astype(jnp.int32)
    unit_pos = (jnp.arange(unit_count, dtype=jnp.int32) * UNIT).astype(jnp.int32)
    unit_doc = lax.optimization_barrier(jnp.sum((doc_ends[:, None, :] <= unit_pos[None, :, None]).astype(jnp.int32), axis=2)).astype(jnp.int32)

    def group_squares(group_item):
        group_acts, group_grads, group_docs = group_item

        def add_unit(carry, unit_item):
            unit_acts, unit_grads, doc_index = unit_item
            product = lax.dot_general(unit_acts, unit_grads, (((0,), (0,)), ((), ())), preferred_element_type=jnp.float32)
            return (carry.at[doc_index].add(product), None)
        start = jnp.zeros((DOCS, D, D), jnp.float32)
        totals, _ = lax.scan(add_unit, start, (group_acts.reshape(unit_count, UNIT, D), group_grads.reshape(unit_count, UNIT, D), group_docs))
        return lax.optimization_barrier(jnp.sum(totals * totals, axis=(1, 2)))
    squares = lax.map(group_squares, (token_acts, token_grads, unit_doc))
    doc_norm = jnp.sqrt(squares)
    threshold = lax.optimization_barrier(jnp.mean(doc_norm, axis=1, keepdims=True))
    doc_ratio = doc_norm / threshold
    clip_factor = 1.0 / jnp.maximum(doc_norm, threshold)
    positions = jnp.arange(PACK, dtype=jnp.int32)
    doc_ids = lax.optimization_barrier(jnp.sum((doc_ends[:, None, :] <= positions[None, :, None]).astype(jnp.int32), axis=2))
    token_clip = jnp.take_along_axis(clip_factor, doc_ids, axis=1)
    scaled = (token_clip[:, :, None] * token_grads.astype(jnp.float32)).astype(jnp.bfloat16)
    gradient = lax.dot_general(token_acts.reshape(TOKENS, D), scaled.reshape(TOKENS, D), (((0,), (0,)), ((), ())), preferred_element_type=jnp.float32)
    gradient = gradient * (D / (N_DP * DOCS))
    grad_tiles = gradient.reshape(ROW_TILES, TILE_R, COL_TILES, TILE_C).transpose(0, 2, 1, 3)
    grad_tiles = grad_tiles.reshape(N_SEQ, TILE_R, TILE_C)
    return (doc_ratio, grad_tiles)
```

```python
import functools

import jax
import jax.numpy as jnp
from jax import lax
from jax.experimental import pallas as pl
from jax.experimental.pallas import tpu as pltpu
from jax.sharding import Mesh, PartitionSpec as P

DOCS = 3
NZ, NY, NC = 8, 4, 2
TOK = 128
BLOCKS = NY * NC
CHUNK = TOK * BLOCKS
TILE = 512
SEQ = ("z", "y", "core")
F32, BF16 = jnp.float32, jnp.bfloat16
MIB = 1 << 20


def ring(n, k):
    return [(i, (i + k) % n) for i in range(n)]


def split_mesh(mesh):
    dp = mesh.devices.shape[0]
    return Mesh(mesh.devices.reshape(dp, NZ, NY, NC), ("dp",) + SEQ)


def params(mib):
    return pltpu.CompilerParams(vmem_limit_bytes=mib * MIB)


def cost(flops, moved):
    return pl.CostEstimate(flops=flops, bytes_accessed=moved, transcendentals=0)


def turn_kernel(*refs):
    out = refs[-1]
    z = pl.program_id(0)
    own, own_c, r, r_c, oa, oa_c, ob, ob_c, l, l_c = refs[:-1]

    def put(rc, ref):
        out[0, :, rc * TOK : (rc + 1) * TOK] = ref[0].T

    for rc, ref in ((0, own), (1, own_c), (2, r), (3, r_c), (6, l), (7, l_c)):
        put(rc, ref)

    @pl.when(z < NZ // 2)
    def _():
        put(4, oa)
        put(5, oa_c)

    @pl.when(z >= NZ // 2)
    def _():
        put(4, ob)
        put(5, ob_c)


def turned(own, own_c, r, r_c, oa, oa_c, ob, ob_c, l, l_c):
    whole = pl.BlockSpec((1, TOK, TILE), lambda z: (z, 0, 0))
    low = pl.BlockSpec((1, TOK, TILE), lambda z: (jnp.minimum(z, NZ // 2 - 1), 0, 0))
    high = pl.BlockSpec((1, TOK, TILE), lambda z: (jnp.maximum(z - NZ // 2, 0), 0, 0))
    return pl.pallas_call(
        turn_kernel,
        grid=(NZ,),
        in_specs=[whole, whole, whole, whole, low, low, high, high, whole, whole],
        out_specs=pl.BlockSpec((1, TILE, CHUNK), lambda z: (z, 0, 0)),
        out_shape=jax.ShapeDtypeStruct((NZ, TILE, CHUNK), BF16),
        compiler_params=params(32),
        cost_estimate=cost(0, 16 * MIB),
        name="turn",
    )(own, own_c, r, r_c, oa, oa_c, ob, ob_c, l, l_c)


def add_chunk(doc_ref, acts_ref, low_ref, high_ref, acc_ref):
    for d in range(DOCS):
        held = [doc_ref[b] == d for b in range(BLOCKS)]
        any_held = functools.reduce(jnp.logical_or, held)

        @pl.when(any_held)
        def _():
            blocks = [low_ref[b] if b < BLOCKS // 2 else high_ref[b - BLOCKS // 2] for b in range(BLOCKS)]
            kept = [jnp.where(h, x, jnp.zeros_like(x)) for h, x in zip(held, blocks)]
            acc_ref[d] += jnp.dot(
                acts_ref[0], jnp.concatenate(kept, axis=0), preferred_element_type=F32
            )


def first_kernel(z_ref, doc_ref, acts_ref, low_ref, high_ref, acc_ref):
    acc_ref[...] = jnp.zeros_like(acc_ref)
    add_chunk(doc_ref, acts_ref, low_ref, high_ref, acc_ref)


def next_kernel(z_ref, doc_ref, acts_ref, low_ref, high_ref, acc_in, acc_ref):
    acc_ref[...] = acc_in[...]
    add_chunk(doc_ref, acts_ref, low_ref, high_ref, acc_ref)


def last_kernel(z_ref, doc_ref, acts_ref, low_ref, high_ref, acc_in, out_ref, acc_ref):
    acc_ref[...] = acc_in[...]
    add_chunk(doc_ref, acts_ref, low_ref, high_ref, acc_ref)
    for d in range(DOCS):
        total = acc_ref[d]
        out_ref[d] = jnp.sum((total * total).reshape(TILE // 8, 8, TILE), axis=0)


def norm_call(kind, z, docs, acts, low, high, acc=None):
    acc_shape = jax.ShapeDtypeStruct((DOCS, TILE, TILE), F32)
    acc_spec = pl.BlockSpec((DOCS, TILE, TILE), lambda i, z, doc: (0, 0, 0))
    half_spec = pl.BlockSpec((BLOCKS // 2, TOK, TILE), lambda i, z, doc: (0, 0, 0))
    in_specs = [
        pl.BlockSpec((1, TILE, CHUNK), lambda i, z, doc: (z[0], 0, 0)),
        half_spec,
        half_spec,
    ]
    operands = [z, docs, acts, low, high]
    scratch = []
    out_shape, out_spec = acc_shape, acc_spec
    if kind == "first":
        kernel = first_kernel
    else:
        operands.append(acc)
        in_specs.append(acc_spec)
        kernel = next_kernel
    if kind == "last":
        kernel = last_kernel
        scratch = [pltpu.VMEM((DOCS, TILE, TILE), F32)]
        out_shape = jax.ShapeDtypeStruct((DOCS, 8, TILE), F32)
        out_spec = pl.BlockSpec((DOCS, 8, TILE), lambda i, z, doc: (0, 0, 0))
    return pl.pallas_call(
        kernel,
        grid_spec=pltpu.PrefetchScalarGridSpec(
            num_scalar_prefetch=2,
            grid=(1,),
            in_specs=in_specs,
            out_specs=out_spec,
            scratch_shapes=scratch,
        ),
        out_shape=out_shape,
        compiler_params=params(40),
        cost_estimate=cost(2 * CHUNK * TILE * TILE, 8 * MIB),
        name="norm_" + kind,
    )(*operands)


def grad_kernel(half, me_ref, z_ref, doc_ref, clip_ref, acts_ref, *refs):
    lows, highs = refs[:NZ], refs[NZ : 2 * NZ]
    outs = refs[2 * NZ : 2 * NZ + 4]
    acts_buf, g_buf, acc_ref, acts_sem, g_sem = refs[2 * NZ + 4 :]
    cols = pl.ds(half * (TILE // 2), TILE // 2)
    copies = []
    for s in range(NZ):
        copies.append(
            (
                pltpu.make_async_copy(acts_ref.at[z_ref[s]], acts_buf.at[s], acts_sem.at[s]),
                pltpu.make_async_copy(
                    lows[s].at[:, :, cols], g_buf.at[s, pl.ds(0, BLOCKS // 2)], g_sem.at[s, 0]
                ),
                pltpu.make_async_copy(
                    highs[s].at[:, :, cols],
                    g_buf.at[s, pl.ds(BLOCKS // 2, BLOCKS // 2)],
                    g_sem.at[s, 1],
                ),
            )
        )
        for copy in copies[-1]:
            copy.start()
    for s in range(NZ):
        for copy in copies[s]:
            copy.wait()
        scaled = [
            (clip_ref[doc_ref[s * BLOCKS + b]] * g_buf[s, b].astype(F32)).astype(BF16)
            for b in range(BLOCKS)
        ]
        product = jnp.dot(
            acts_buf[s], jnp.concatenate(scaled, axis=0), preferred_element_type=F32
        )
        if s == 0:
            acc_ref[...] = product
        else:
            acc_ref[...] += product
    for k in range(4):
        start = pl.multiple_of(lax.rem(me_ref[0] + k, 4) * TOK, TOK)
        outs[k][...] = acc_ref[pl.ds(start, TOK), :]


def grad_call(half, me, z_list, docs, clip, acts, lows, highs):
    smem = pl.BlockSpec(memory_space=pltpu.SMEM)
    hbm = pl.BlockSpec(memory_space=pl.ANY)
    return pl.pallas_call(
        functools.partial(grad_kernel, half),
        in_specs=[smem] * 4 + [hbm] * (1 + 2 * NZ),
        out_specs=[pl.BlockSpec(memory_space=pltpu.VMEM)] * 4,
        out_shape=[jax.ShapeDtypeStruct((TOK, TILE // 2), F32)] * 4,
        scratch_shapes=[
            pltpu.VMEM((NZ, TILE, CHUNK), BF16),
            pltpu.VMEM((NZ, BLOCKS, TOK, TILE // 2), BF16),
            pltpu.VMEM((TILE, TILE // 2), F32),
            pltpu.SemaphoreType.DMA((NZ,)),
            pltpu.SemaphoreType.DMA((NZ, 2)),
        ],
        compiler_params=params(40),
        cost_estimate=cost(NZ * CHUNK * TILE * TILE, 12 * MIB),
        name="grad",
    )(me, z_list, docs, clip, acts, *lows, *highs)


def body(hidden_states, q_grads, doc_units):
    me, z = lax.axis_index("dp"), lax.axis_index("z")
    y, core = lax.axis_index("y"), lax.axis_index("core")

    def at(array, index, axis=0):
        return lax.dynamic_index_in_dim(array, index, axis, keepdims=False)

    grads = q_grads.reshape(TOK, NY, NC, TILE).transpose(2, 1, 0, 3)
    kept, given = at(grads, core), at(grads, 1 - core)
    got = lax.ppermute(given, "core", ring(NC, 1))
    pair = jnp.stack([kept, got], axis=1)
    near = {k: lax.ppermute(at(pair, (y + k) % NY), "y", ring(NY, k)) for k in (2, 1, 3)}
    low = jnp.concatenate([at(pair, y), near[1]], axis=0)
    high = jnp.concatenate([near[2], near[3]], axis=0)

    acts = hidden_states.reshape(TOK, NZ, TILE).transpose(1, 0, 2)
    acts = lax.all_to_all(acts, "z", split_axis=0, concat_axis=0, tiled=True)
    right = lax.ppermute(acts, "y", ring(NY, 1))
    left = lax.ppermute(acts, "y", ring(NY, -1))
    far_a = lax.ppermute(right[: NZ // 2], "y", ring(NY, 1))
    far_b = lax.ppermute(left[NZ // 2 :], "y", ring(NY, -1))
    shards = []
    for shard in (acts, right, far_a, far_b, left):
        shards += [shard, lax.ppermute(shard, "core", ring(NC, 1))]
    acts_t = turned(*shards)

    doc_ends = jnp.cumsum(doc_units[0])
    steps = jnp.array([0, -1, 1, -2, 2, -3, 3, 4], jnp.int32)
    z_list = (z + steps) % NZ
    across = jnp.array([0, -1, -2, -3], jnp.int32)
    units = (
        z_list[:, None, None] * BLOCKS
        + ((y + across) % NY)[None, :, None] * NC
        + jnp.stack([core, 1 - core])[None, None, :]
    ).reshape(NZ, BLOCKS)
    docs = jnp.sum((doc_ends <= units[:, :, None]).astype(jnp.int32), axis=2)

    lows, highs = {0: low}, {0: high}
    for half in (lows, highs):
        to_right = to_left = half[0]
        for s in range(1, NZ // 2):
            to_right = lax.ppermute(to_right, "z", ring(NZ, 1))
            to_left = lax.ppermute(to_left, "z", ring(NZ, -1))
            half[-s], half[s] = to_right, to_left
        if half is lows:
            half[NZ // 2] = lax.ppermute(to_right, "z", ring(NZ, 1))
        else:
            half[NZ // 2] = lax.ppermute(to_left, "z", ring(NZ, -1))
    order = (0, -1, 1, -2, 2, -3, 3, 4)
    lows, highs = [lows[s] for s in order], [highs[s] for s in order]

    acc = None
    for s in range(NZ):
        kind = "first" if s == 0 else "last" if s == NZ - 1 else "next"
        acc = norm_call(kind, z_list[s : s + 1], docs[s], acts_t, lows[s], highs[s], acc)
    partial = jnp.sum(acc, axis=(1, 2))
    sent = jnp.broadcast_to(partial[None, :, None], (NZ * BLOCKS, DOCS, 128))
    came = lax.all_to_all(sent, SEQ, split_axis=0, concat_axis=0, tiled=True)
    doc_norm = jnp.sqrt(jnp.sum(came[:, :, 0], axis=0))
    threshold = jnp.mean(doc_norm)
    doc_ratio = doc_norm / threshold
    clip = 1.0 / jnp.maximum(doc_norm, threshold)

    halves = []
    for half in range(2):
        parts = grad_call(
            half, me.reshape(1), z_list, docs.reshape(-1), clip, acts_t, lows, highs
        )
        total = parts[0]
        for k in (2, 1, 3):
            total = total + lax.ppermute(parts[k], "dp", ring(4, k))
        halves.append(total)
    clipped = jnp.concatenate(halves, axis=1) * (4096 / 12)
    return (doc_ratio[None, :], clipped[None])


def solution(mesh):
    in_specs = (P(("dp",) + SEQ, None), P(("dp",) + SEQ, None), P("dp", None))
    out_specs = (P("dp", None), P(SEQ, "dp", None))
    return jax.shard_map(
        body, mesh=split_mesh(mesh), in_specs=in_specs, out_specs=out_specs, check_vma=False
    )
```

```python
import functools

import jax
import jax.numpy as jnp
from jax import lax
from jax.experimental import pallas as pl
from jax.experimental.pallas import tpu as pltpu
from jax.sharding import Mesh, PartitionSpec as P

DOCS = 3
NZ, NY, NC = 8, 4, 2
TOK = 128
BLOCKS = NY * NC
CHUNK = TOK * BLOCKS
TILE = 512
WIDE = TILE // 2
LANES = 128
MEMBERS = NZ * BLOCKS
SEQ = ("z", "y", "core")
F32, BF16 = jnp.float32, jnp.bfloat16
MIB = 1 << 20
STEPS = (0, -1, 1, -2, 2, -3, 3, 4)
VMEM = pl.BlockSpec(memory_space=pltpu.VMEM)
SMEM = pl.BlockSpec(memory_space=pltpu.SMEM)
ANY = pl.BlockSpec(memory_space=pl.ANY)


def in_hbm(x):
    return pltpu.with_memory_space_constraint(x, pltpu.HBM)


def ring(n, k):
    return [(i, (i + k) % n) for i in range(n)]


def split_mesh(mesh):
    dp = mesh.devices.shape[0]
    return Mesh(mesh.devices.reshape(dp, NZ, NY, NC), ("dp",) + SEQ)


def params(mib):
    return pltpu.CompilerParams(vmem_limit_bytes=mib * MIB)


def cost(flops, moved):
    return pl.CostEstimate(flops=flops, bytes_accessed=moved, transcendentals=0)


def open_acts_kernel(acts_ref, units_in, out_ref, z_ref, doc_ref, buf, units_ref, sem, units_sem):
    fetch = pltpu.make_async_copy(units_in, units_ref, units_sem)
    fetch.start()
    copies = [
        pltpu.make_async_copy(acts_ref.at[:, pl.ds(i * TILE, TILE)], buf.at[i], sem.at[i])
        for i in range(NZ)
    ]
    for copy in copies:
        copy.start()
    fetch.wait()
    z, y, core = (lax.axis_index(a) for a in SEQ)
    first_end = units_ref[0, 0]
    second_end = first_end + units_ref[0, 1]
    for s, step in enumerate(STEPS):
        there = lax.rem(z + (step + NZ), NZ)
        z_ref[s] = there
        for b in range(BLOCKS):
            unit = there * BLOCKS + lax.rem(y + (NY - b // NC), NY) * NC + (core if b % NC == 0 else 1 - core)
            doc_ref[s * BLOCKS + b] = (unit >= first_end).astype(jnp.int32) + (
                unit >= second_end
            ).astype(jnp.int32)
    for i in range(NZ):
        copies[i].wait()
        out_ref[i] = buf[i].T


def open_acts(acts, units):
    return pl.pallas_call(
        open_acts_kernel,
        in_specs=[ANY, ANY],
        out_specs=[VMEM, SMEM, SMEM],
        out_shape=[
            jax.ShapeDtypeStruct((NZ, TILE, TOK), BF16),
            jax.ShapeDtypeStruct((NZ,), jnp.int32),
            jax.ShapeDtypeStruct((MEMBERS,), jnp.int32),
        ],
        scratch_shapes=[
            pltpu.VMEM((NZ, TOK, TILE), BF16),
            pltpu.SMEM((1, DOCS), jnp.int32),
            pltpu.SemaphoreType.DMA((NZ,)),
            pltpu.SemaphoreType.DMA,
        ],
        compiler_params=params(8),
        cost_estimate=cost(0, 2 * MIB),
        name="open_acts",
    )(in_hbm(acts), in_hbm(units))


def open_grads_kernel(grads_ref, kept_ref, given_ref, sem):
    y, core = lax.axis_index("y"), lax.axis_index("core")
    copies = []
    for j, (out, c) in enumerate(((given_ref, 1 - core), (kept_ref, core))):
        for k in range(NY):
            tile = lax.rem(y + k, NY) * NC + c
            for h in range(2):
                cols = pl.ds(pl.multiple_of(tile * TILE + h * WIDE, WIDE), WIDE)
                copies.append(
                    pltpu.make_async_copy(grads_ref.at[:, cols], out.at[k, h], sem.at[j, k, h])
                )
    for copy in copies:
        copy.start()
    for copy in copies:
        copy.wait()


def open_grads(grads):
    shape = jax.ShapeDtypeStruct((NY, 2, TOK, WIDE), BF16)
    return pl.pallas_call(
        open_grads_kernel,
        in_specs=[ANY],
        out_specs=[VMEM] * 2,
        out_shape=[shape] * 2,
        scratch_shapes=[pltpu.SemaphoreType.DMA((NC, NY, 2))],
        compiler_params=params(4),
        cost_estimate=cost(0, 2 * MIB),
        name="open_grads",
    )(in_hbm(grads))


def pair_kernel(kept_ref, got_ref, *outs):
    for k in range(NY):
        for h in range(2):
            outs[k][h, 0] = kept_ref[k, h]
            outs[k][h, 1] = got_ref[k, h]


def pair_up(kept, got):
    return pl.pallas_call(
        pair_kernel,
        in_specs=[VMEM] * 2,
        out_specs=[VMEM] * NY,
        out_shape=[jax.ShapeDtypeStruct((2, NC, TOK, WIDE), BF16)] * NY,
        compiler_params=params(8),
        cost_estimate=cost(0, 2 * MIB),
        name="pair_up",
    )(kept, got)


def join_kernel(*refs):
    for h in range(2):
        for k in range(NY):
            refs[NY][h, k * NC : (k + 1) * NC] = refs[k][h]


def join(pairs):
    return pl.pallas_call(
        join_kernel,
        in_specs=[VMEM] * NY,
        out_specs=VMEM,
        out_shape=jax.ShapeDtypeStruct((2, BLOCKS, TOK, WIDE), BF16),
        compiler_params=params(8),
        cost_estimate=cost(0, 2 * MIB),
        name="join",
    )(*pairs)


PIECES = (
    (0, 0, TILE),
    (1, 0, TILE),
    (2, 0, TILE),
    (3, 0, TILE),
    (4, 0, WIDE),
    (4, WIDE, WIDE),
    (5, 0, WIDE),
    (5, WIDE, WIDE),
    (6, 0, TILE),
    (7, 0, TILE),
)
ACTS = len(PIECES)


def acts_copies(acts, z, buf, sem):
    return [
        pltpu.make_async_copy(ref.at[z], buf.at[b, pl.ds(row, rows)], sem.at[i])
        for i, (ref, (b, row, rows)) in enumerate(zip(acts, PIECES))
    ]


def side_by_side(buf):
    return jnp.concatenate([buf[b] for b in range(BLOCKS)], axis=1)


def norm_kernel(chunks, has_acc, is_last, z_ref, doc_ref, *refs):
    n = len(chunks)
    acts, refs = refs[:ACTS], refs[ACTS:]
    many = 2 if is_last else n
    grads, refs = refs[:many], refs[many:]
    if has_acc and not is_last:
        refs = refs[1:]
    acc_ref, refs = refs[0], refs[1:]
    if is_last:
        out_ref, refs = refs[0], refs[1:]
        acts_buf, sem = refs
    else:
        acts_buf, grads_buf, sem = refs
    copies = []
    for i, s in enumerate(chunks):
        copies.append(acts_copies(acts, z_ref[s], acts_buf.at[i], sem.at[i]))
        if not is_last:
            copies[-1].append(
                pltpu.make_async_copy(grads[i], grads_buf.at[i], sem.at[i, ACTS])
            )
    for several in copies:
        for copy in several:
            copy.start()
    if not has_acc:
        acc_ref[...] = jnp.zeros_like(acc_ref)
    for i, s in enumerate(chunks):
        for copy in copies[i]:
            copy.wait()
        for d in range(DOCS):
            held = [doc_ref[s * BLOCKS + b] == d for b in range(BLOCKS)]

            @pl.when(functools.reduce(jnp.logical_or, held))
            def _():
                x = side_by_side(acts_buf.at[i])
                for h in range(2):
                    g = grads[h] if is_last else grads_buf.at[i, h]
                    kept = [
                        jnp.where(held[b], g[b], jnp.zeros((TOK, WIDE), BF16))
                        for b in range(BLOCKS)
                    ]
                    acc_ref[d, :, h * WIDE : (h + 1) * WIDE] += jnp.dot(
                        x, jnp.concatenate(kept, axis=0), preferred_element_type=F32
                    )

    if is_last:
        lane = lax.broadcasted_iota(jnp.int32, (1, LANES), 1)
        row = jnp.zeros((1, LANES), F32)
        for d in range(DOCS):
            total = acc_ref[d]
            row = jnp.where(lane == d, jnp.sum(total * total), row)
        out_ref[...] = jnp.broadcast_to(row[None], out_ref.shape)


def norm_call(chunks, z_list, docs, acts, grads, acc=None, is_last=False):
    n = len(chunks)
    operands = [z_list, docs, *map(in_hbm, acts)]
    for s in chunks:
        operands += grads[s] if is_last else [in_hbm(grads[s])]
    in_specs = [SMEM] * 2 + [ANY] * ACTS + ([VMEM] * 2 if is_last else [ANY] * n)
    aliases = {}
    if acc is not None:
        operands.append(acc)
        in_specs.append(VMEM)
        if not is_last:
            aliases = {len(operands) - 1: 0}
    scratch = [pltpu.VMEM((n, BLOCKS, TILE, TOK), BF16)]
    if is_last:
        out_shape = jax.ShapeDtypeStruct((MEMBERS, 1, LANES), F32)
    else:
        out_shape = jax.ShapeDtypeStruct((DOCS, TILE, TILE), F32)
        scratch.append(pltpu.VMEM((n, 2, BLOCKS, TOK, WIDE), BF16))
    return pl.pallas_call(
        functools.partial(norm_kernel, chunks, acc is not None, is_last),
        in_specs=in_specs,
        out_specs=VMEM,
        out_shape=out_shape,
        input_output_aliases=aliases,
        scratch_shapes=scratch + [pltpu.SemaphoreType.DMA((n, ACTS + 2))],
        compiler_params=params(12 + 2 * n),
        cost_estimate=cost(2 * n * CHUNK * TILE * TILE, 3 * n * MIB),
        name="norm_" + "_".join(str(s) for s in chunks),
    )(*operands)


def grad_kernel(z_ref, doc_ref, norm_ref, *refs):
    acts, refs = refs[:ACTS], refs[ACTS:]
    grads, refs = refs[: NZ + 1], refs[NZ + 1 :]
    outs, ratio_ref, acc_ref, acts_buf, grads_buf, sem = refs[:4], *refs[4:]
    copies = []
    for s in range(NZ):
        if s < NZ - 1:
            pieces = [(grads[s], grads_buf.at[s])]
        else:
            pieces = [(grads[s + h], grads_buf.at[s, h]) for h in range(2)]
        copies.append(
            [
                pltpu.make_async_copy(src, dst, sem.at[s, ACTS + i])
                for i, (src, dst) in enumerate(pieces)
            ]
            + acts_copies(acts, z_ref[s], acts_buf.at[s], sem.at[s])
        )
        for copy in copies[s]:
            copy.start()
    squares = jnp.sum(norm_ref[...], axis=0)
    doc_norm = jnp.where(squares > 0, jnp.sqrt(squares), 0)
    lane = lax.broadcasted_iota(jnp.int32, (1, LANES), 1)
    threshold = jnp.sum(doc_norm, axis=1, keepdims=True) / DOCS
    ratio_ref[...] = doc_norm / threshold
    factor = 1.0 / jnp.maximum(doc_norm, threshold)
    clip = [jnp.sum(jnp.where(lane == d, factor, 0)) for d in range(DOCS)]
    for s in range(NZ):
        for copy in copies[s]:
            copy.wait()
        for h in range(2):
            scaled = []
            for b in range(BLOCKS):
                doc = doc_ref[s * BLOCKS + b]
                mine = jnp.where(doc == 0, clip[0], jnp.where(doc == 1, clip[1], clip[2]))
                scaled.append((mine * grads_buf[s, h, b].astype(F32)).astype(BF16))
            product = jnp.dot(
                side_by_side(acts_buf.at[s]),
                jnp.concatenate(scaled, axis=0),
                preferred_element_type=F32,
            )
            cols = slice(h * WIDE, (h + 1) * WIDE)
            if s == 0:
                acc_ref[:, cols] = product
            else:
                acc_ref[:, cols] += product
    me = lax.axis_index("dp")
    for k in range(4):
        first = pl.multiple_of(lax.rem(me + k, 4) * TOK, TOK)
        outs[k][...] = acc_ref[pl.ds(first, TOK), :]


def grad_call(z_list, docs, norms, acts, grads):
    operands = [z_list, docs, norms, *map(in_hbm, acts)]
    operands += map(in_hbm, [*grads[:-1], *grads[-1]])
    return pl.pallas_call(
        grad_kernel,
        in_specs=[SMEM] * 2 + [VMEM] + [ANY] * (ACTS + NZ + 1),
        out_specs=[VMEM] * 5,
        out_shape=[jax.ShapeDtypeStruct((TOK, TILE), F32)] * 4
        + [jax.ShapeDtypeStruct((1, LANES), F32)],
        scratch_shapes=[
            pltpu.VMEM((TILE, TILE), F32),
            pltpu.VMEM((NZ, BLOCKS, TILE, TOK), BF16),
            pltpu.VMEM((NZ, 2, BLOCKS, TOK, WIDE), BF16),
            pltpu.SemaphoreType.DMA((NZ, ACTS + 2)),
        ],
        compiler_params=params(32),
        cost_estimate=cost(2 * NZ * CHUNK * TILE * TILE, 18 * MIB),
        name="grad",
    )(*operands)


def body(hidden_states, q_grads, doc_units):
    def after(x, *done):
        return lax.optimization_barrier((x, *done))[0]

    def move(x, axis, k):
        return lax.ppermute(x, axis, ring(lax.axis_size(axis), k))


    kept, given = open_grads(q_grads)
    got = move(given, "core", 1)
    pair = pair_up(kept, got)
    near = {k: move(pair[k], "y", k) for k in (2, 1, 3)}
    here = join([pair[0], near[1], near[2], near[3]])

    acts_t, z_list, docs = open_acts(hidden_states, doc_units)
    own = lax.all_to_all(acts_t, "z", split_axis=0, concat_axis=0, tiled=True)

    g = {0: here}
    right, left = move(own, "y", 1), move(own, "y", -1)
    own_c = move(own, "core", 1)
    for s in (1, 2):
        g[-s], g[s] = move(g[1 - s], "z", 1), move(g[s - 1], "z", -1)
    g[-3] = move(after(g[-2], right, left), "z", 1)
    g[3] = move(after(g[2], right, left), "z", -1)
    far = [move(right[:, :WIDE], "y", 1), move(left[:, WIDE:], "y", -1)]
    right_c, left_c = move(right, "core", 1), move(left, "core", 1)
    last = [
        move(after(g[-3][0], *far, right_c, left_c), "z", 1),
        move(after(g[3][1], *far, right_c, left_c), "z", -1),
    ]
    acts = [own, own_c, right, right_c, *far, *(move(x, "core", 1) for x in far), left, left_c]
    chunks = [g[s] for s in STEPS[:-1]] + [last]
    acc = norm_call((0, 1, 2, 3, 4, 5, 6), z_list, docs, acts, chunks)
    partial = norm_call((7,), z_list, docs, acts, chunks, acc, is_last=True)
    norms = lax.all_to_all(partial, SEQ, split_axis=0, concat_axis=0, tiled=True)

    *parts, ratio = grad_call(z_list, docs, norms, acts, chunks)
    total = parts[0]
    for k in (2, 1, 3):
        total = total + move(parts[k], "dp", k)
    return (ratio[:, :DOCS], (total * (4096 / 12))[None])


def solution(mesh):
    in_specs = (P(("dp",) + SEQ, None), P(("dp",) + SEQ, None), P("dp", None))
    out_specs = (P("dp", None), P(SEQ, "dp", None))
    return jax.shard_map(
        body, mesh=split_mesh(mesh), in_specs=in_specs, out_specs=out_specs, check_vma=False
    )
```

```python
import functools

import jax
import jax.numpy as jnp
from jax import lax
from jax.experimental import pallas as pl
from jax.experimental.pallas import tpu as pltpu
from jax.sharding import Mesh, PartitionSpec as P

DOCS = 3
NZ, NY, NC = 8, 4, 2
TOK = 128
BLOCKS = NY * NC
CHUNK = TOK * BLOCKS
TILE = 512
WIDE = TILE // 2
LANES = 128
MEMBERS = NZ * BLOCKS
PARTS = 2 * BLOCKS
CUT = 7
SEQ = ("z", "y", "core")
F32, BF16 = jnp.float32, jnp.bfloat16
MIB = 1 << 20
STEPS = (0, -1, 1, -2, 2, -3, 3, 4)
VMEM = pl.BlockSpec(memory_space=pltpu.VMEM)
SMEM = pl.BlockSpec(memory_space=pltpu.SMEM)
ANY = pl.BlockSpec(memory_space=pl.ANY)


def in_hbm(x):
    return pltpu.with_memory_space_constraint(x, pltpu.HBM)


def ring(n, k):
    return [(i, (i + k) % n) for i in range(n)]


def split_mesh(mesh):
    dp = mesh.devices.shape[0]
    return Mesh(mesh.devices.reshape(dp, NZ, NY, NC), ("dp",) + SEQ)


def params(mib):
    return pltpu.CompilerParams(vmem_limit_bytes=mib * MIB)


def cost(flops, moved):
    return pl.CostEstimate(flops=flops, bytes_accessed=moved, transcendentals=0)


def open_acts_kernel(acts_ref, units_in, out_ref, z_ref, doc_ref, buf, units_ref, sem, units_sem):
    fetch = pltpu.make_async_copy(units_in, units_ref, units_sem)
    fetch.start()
    copies = [
        pltpu.make_async_copy(acts_ref.at[:, pl.ds(i * TILE, TILE)], buf.at[i], sem.at[i])
        for i in range(NZ)
    ]
    for copy in copies:
        copy.start()
    fetch.wait()
    z, y, core = (lax.axis_index(a) for a in SEQ)
    first_end = units_ref[0, 0]
    second_end = first_end + units_ref[0, 1]
    for s, step in enumerate(STEPS):
        there = lax.rem(z + (step + NZ), NZ)
        z_ref[s] = there
        for b in range(BLOCKS):
            unit = there * BLOCKS + lax.rem(y + (NY - b // NC), NY) * NC + (core if b % NC == 0 else 1 - core)
            doc_ref[s * BLOCKS + b] = (unit >= first_end).astype(jnp.int32) + (
                unit >= second_end
            ).astype(jnp.int32)
    for i in range(NZ):
        copies[i].wait()
        out_ref[i] = buf[i].T


def open_acts(acts, units):
    return pl.pallas_call(
        open_acts_kernel,
        in_specs=[ANY, ANY],
        out_specs=[VMEM, SMEM, SMEM],
        out_shape=[
            jax.ShapeDtypeStruct((NZ, TILE, TOK), BF16),
            jax.ShapeDtypeStruct((NZ,), jnp.int32),
            jax.ShapeDtypeStruct((MEMBERS,), jnp.int32),
        ],
        scratch_shapes=[
            pltpu.VMEM((NZ, TOK, TILE), BF16),
            pltpu.SMEM((1, DOCS), jnp.int32),
            pltpu.SemaphoreType.DMA((NZ,)),
            pltpu.SemaphoreType.DMA,
        ],
        compiler_params=params(8),
        cost_estimate=cost(0, 2 * MIB),
        name="open_acts",
    )(in_hbm(acts), in_hbm(units))


def open_grads_kernel(grads_ref, kept_ref, given_ref, sem):
    y, core = lax.axis_index("y"), lax.axis_index("core")
    copies = []
    for j, (out, c) in enumerate(((given_ref, 1 - core), (kept_ref, core))):
        for k in range(NY):
            tile = lax.rem(y + k, NY) * NC + c
            for h in range(2):
                cols = pl.ds(pl.multiple_of(tile * TILE + h * WIDE, WIDE), WIDE)
                copies.append(
                    pltpu.make_async_copy(grads_ref.at[:, cols], out.at[k, h], sem.at[j, k, h])
                )
    for copy in copies:
        copy.start()
    for copy in copies:
        copy.wait()


def open_grads(grads):
    shape = jax.ShapeDtypeStruct((NY, 2, TOK, WIDE), BF16)
    return pl.pallas_call(
        open_grads_kernel,
        in_specs=[ANY],
        out_specs=[VMEM] * 2,
        out_shape=[shape] * 2,
        scratch_shapes=[pltpu.SemaphoreType.DMA((NC, NY, 2))],
        compiler_params=params(4),
        cost_estimate=cost(0, 2 * MIB),
        name="open_grads",
    )(in_hbm(grads))


def pair_kernel(kept_ref, got_ref, *outs):
    for k in range(NY):
        for h in range(2):
            outs[k][h, 0] = kept_ref[k, h]
            outs[k][h, 1] = got_ref[k, h]


def pair_up(kept, got):
    return pl.pallas_call(
        pair_kernel,
        in_specs=[VMEM] * 2,
        out_specs=[VMEM] * NY,
        out_shape=[jax.ShapeDtypeStruct((2, NC, TOK, WIDE), BF16)] * NY,
        compiler_params=params(8),
        cost_estimate=cost(0, 2 * MIB),
        name="pair_up",
    )(kept, got)


def join_kernel(*refs):
    for h in range(2):
        for k in range(NY):
            refs[NY][pl.ds(h * BLOCKS + k * NC, NC)] = refs[k][h]


def join(pairs):
    return pl.pallas_call(
        join_kernel,
        in_specs=[VMEM] * NY,
        out_specs=VMEM,
        out_shape=jax.ShapeDtypeStruct((PARTS, TOK, WIDE), BF16),
        compiler_params=params(8),
        cost_estimate=cost(0, 2 * MIB),
        name="join",
    )(*pairs)


PIECES = (
    (0, 0, TILE),
    (1, 0, TILE),
    (2, 0, TILE),
    (3, 0, TILE),
    (4, 0, WIDE),
    (4, WIDE, WIDE),
    (5, 0, WIDE),
    (5, WIDE, WIDE),
    (6, 0, TILE),
    (7, 0, TILE),
)
ACTS = len(PIECES)


def acts_copies(acts, z, buf, sem):
    return [
        pltpu.make_async_copy(ref.at[z], buf.at[b, pl.ds(row, rows)], sem.at[i])
        for i, (ref, (b, row, rows)) in enumerate(zip(acts, PIECES))
    ]


def part_of(parts, h, b):
    i = h * BLOCKS + b
    if len(parts) == 1:
        return parts[0][i]
    return parts[0][i] if i < CUT else parts[1][i - CUT]


def side_by_side(buf):
    return jnp.concatenate([buf[b] for b in range(BLOCKS)], axis=1)


def norm_kernel(chunks, is_last, z_ref, doc_ref, *refs):
    n = len(chunks)
    many = 2 if is_last else n
    if is_last:
        late_ref, refs = refs[0], refs[1:]
    else:
        acts, refs = refs[:ACTS], refs[ACTS:]
    grads, refs = refs[:many], refs[many:]
    acc_ref, refs = refs[0], refs[1:]
    if is_last:
        (out_ref,) = refs
    else:
        late_ref, acts_buf, grads_buf, sem = refs
    copies = []
    for i, s in enumerate(chunks):
        copies.append([])
        if not is_last:
            copies[-1] += acts_copies(acts, z_ref[s], acts_buf.at[i], sem.at[i])
            copies[-1].append(
                pltpu.make_async_copy(grads[i], grads_buf.at[i], sem.at[i, ACTS])
            )
    for several in copies:
        for copy in several:
            copy.start()
    if not is_last:
        late_copies = acts_copies(acts, z_ref[NZ - 1], late_ref, sem.at[n])
        for copy in late_copies:
            copy.start()
        acc_ref[...] = jnp.zeros_like(acc_ref)
    for i, s in enumerate(chunks):
        for copy in copies[i]:
            copy.wait()
        for d in range(DOCS):
            held = [doc_ref[s * BLOCKS + b] == d for b in range(BLOCKS)]

            @pl.when(functools.reduce(jnp.logical_or, held))
            def _():
                x = side_by_side(late_ref if is_last else acts_buf.at[i])
                for h in range(2):
                    parts = grads if is_last else (grads_buf.at[i],)
                    kept = [
                        jnp.where(held[b], part_of(parts, h, b), jnp.zeros((TOK, WIDE), BF16))
                        for b in range(BLOCKS)
                    ]
                    acc_ref[d, :, h * WIDE : (h + 1) * WIDE] += jnp.dot(
                        x, jnp.concatenate(kept, axis=0), preferred_element_type=F32
                    )

    if not is_last:
        for copy in late_copies:
            copy.wait()
    else:
        lane = lax.broadcasted_iota(jnp.int32, (1, LANES), 1)
        row = jnp.zeros((1, LANES), F32)
        for d in range(DOCS):
            total = acc_ref[d]
            row = jnp.where(lane == d, jnp.sum(total * total), row)
        out_ref[...] = jnp.broadcast_to(row[None], out_ref.shape)


def norm_call(chunks, z_list, docs, acts, grads, sums=None):
    n = len(chunks)
    is_last = sums is not None
    operands = [z_list, docs]
    if is_last:
        acc, late = sums
        operands += [late, *grads[chunks[0]], acc]
        out_shape = jax.ShapeDtypeStruct((MEMBERS, 1, LANES), F32)
        scratch = []
    else:
        operands += map(in_hbm, [*acts, *(grads[s] for s in chunks)])
        out_shape = [
            jax.ShapeDtypeStruct((DOCS, TILE, TILE), F32),
            jax.ShapeDtypeStruct((BLOCKS, TILE, TOK), BF16),
        ]
        scratch = [
            pltpu.VMEM((n, BLOCKS, TILE, TOK), BF16),
            pltpu.VMEM((n, PARTS, TOK, WIDE), BF16),
            pltpu.SemaphoreType.DMA((n + 1, ACTS + 2)),
        ]
    return pl.pallas_call(
        functools.partial(norm_kernel, chunks, is_last),
        in_specs=[SMEM] * 2 + [VMEM if is_last else ANY] * (len(operands) - 2),
        out_specs=VMEM if is_last else [VMEM] * 2,
        out_shape=out_shape,
        scratch_shapes=scratch,
        compiler_params=params(12 + 2 * n),
        cost_estimate=cost(2 * n * CHUNK * TILE * TILE, 3 * n * MIB),
        name="norm_" + "_".join(str(s) for s in chunks),
    )(*operands)


def grad_kernel(z_ref, doc_ref, norm_ref, *refs):
    acts, refs = refs[:ACTS], refs[ACTS:]
    grads, refs = refs[: NZ - 1], refs[NZ - 1 :]
    late_acts, late_grads, refs = refs[0], refs[1:3], refs[3:]
    outs, ratio_ref, acc_ref, acts_buf, grads_buf, sem = refs[:4], *refs[4:]
    copies = []
    for s in range(NZ - 1):
        copies.append(
            [pltpu.make_async_copy(grads[s], grads_buf.at[s], sem.at[s, ACTS])]
            + acts_copies(acts, z_ref[s], acts_buf.at[s], sem.at[s])
        )
        for copy in copies[s]:
            copy.start()
    squares = jnp.sum(norm_ref[...], axis=0)
    doc_norm = jnp.where(squares > 0, jnp.sqrt(squares), 0)
    lane = lax.broadcasted_iota(jnp.int32, (1, LANES), 1)
    threshold = jnp.sum(doc_norm, axis=1, keepdims=True) / DOCS
    ratio_ref[...] = doc_norm / threshold
    factor = 1.0 / jnp.maximum(doc_norm, threshold)
    clip = [jnp.sum(jnp.where(lane == d, factor, 0)) for d in range(DOCS)]
    for s in (NZ - 1, *range(NZ - 1)):
        if s < NZ - 1:
            for copy in copies[s]:
                copy.wait()
        parts = (grads_buf.at[s],) if s < NZ - 1 else late_grads
        x = side_by_side(acts_buf.at[s] if s < NZ - 1 else late_acts)
        for h in range(2):
            scaled = []
            for b in range(BLOCKS):
                doc = doc_ref[s * BLOCKS + b]
                mine = jnp.where(doc == 0, clip[0], jnp.where(doc == 1, clip[1], clip[2]))
                scaled.append((mine * part_of(parts, h, b).astype(F32)).astype(BF16))
            product = jnp.dot(
                x,
                jnp.concatenate(scaled, axis=0),
                preferred_element_type=F32,
            )
            cols = slice(h * WIDE, (h + 1) * WIDE)
            if s == NZ - 1:
                acc_ref[:, cols] = product
            else:
                acc_ref[:, cols] += product
    me = lax.axis_index("dp")
    for k in range(4):
        first = pl.multiple_of(lax.rem(me + k, 4) * TOK, TOK)
        outs[k][...] = acc_ref[pl.ds(first, TOK), :]


def grad_call(z_list, docs, norms, acts, grads, late):
    operands = [z_list, docs, norms, *map(in_hbm, acts)]
    operands += map(in_hbm, grads[:-1])
    operands += [late, *grads[-1]]
    return pl.pallas_call(
        grad_kernel,
        in_specs=[SMEM] * 2 + [VMEM] + [ANY] * (ACTS + NZ - 1) + [VMEM] * 3,
        out_specs=[VMEM] * 5,
        out_shape=[jax.ShapeDtypeStruct((TOK, TILE), F32)] * 4
        + [jax.ShapeDtypeStruct((1, LANES), F32)],
        scratch_shapes=[
            pltpu.VMEM((TILE, TILE), F32),
            pltpu.VMEM((NZ - 1, BLOCKS, TILE, TOK), BF16),
            pltpu.VMEM((NZ - 1, PARTS, TOK, WIDE), BF16),
            pltpu.SemaphoreType.DMA((NZ - 1, ACTS + 1)),
        ],
        compiler_params=params(32),
        cost_estimate=cost(2 * NZ * CHUNK * TILE * TILE, 18 * MIB),
        name="grad",
    )(*operands)


def body(hidden_states, q_grads, doc_units):
    def after(x, *done):
        return lax.optimization_barrier((x, *done))[0]

    def move(x, axis, k):
        return lax.ppermute(x, axis, ring(lax.axis_size(axis), k))


    kept, given = open_grads(q_grads)
    got = move(given, "core", 1)
    pair = pair_up(kept, got)
    near = {k: move(pair[k], "y", k) for k in (2, 1, 3)}
    here = join([pair[0], near[1], near[2], near[3]])

    acts_t, z_list, docs = open_acts(hidden_states, doc_units)
    own = lax.all_to_all(acts_t, "z", split_axis=0, concat_axis=0, tiled=True)

    g = {0: here}
    right, left = move(own, "y", 1), move(own, "y", -1)
    own_c = move(own, "core", 1)
    for s in (1, 2):
        g[-s], g[s] = move(g[1 - s], "z", 1), move(g[s - 1], "z", -1)
    g[-3] = move(after(g[-2], right, left), "z", 1)
    g[3] = move(after(g[2], right, left), "z", -1)
    far = [move(right[:, :WIDE], "y", 1), move(left[:, WIDE:], "y", -1)]
    right_c, left_c = move(right, "core", 1), move(left, "core", 1)
    last = [
        move(after(g[-3][:CUT], *far, right_c, left_c), "z", 1),
        move(after(g[3][CUT:], *far, right_c, left_c), "z", -1),
    ]
    acts = [own, own_c, right, right_c, *far, *(move(x, "core", 1) for x in far), left, left_c]
    chunks = [g[s] for s in STEPS[:-1]] + [last]
    sums = norm_call((0, 1, 2, 3, 4, 5, 6), z_list, docs, acts, chunks)
    partial = norm_call((7,), z_list, docs, acts, chunks, sums)
    norms = lax.all_to_all(partial, SEQ, split_axis=0, concat_axis=0, tiled=True)

    *parts, ratio = grad_call(z_list, docs, norms, acts, chunks, sums[1])
    total = parts[0]
    for k in (2, 1, 3):
        total = total + move(parts[k], "dp", k)
    return (ratio[:, :DOCS], (total * (4096 / 12))[None])


def solution(mesh):
    in_specs = (P(("dp",) + SEQ, None), P(("dp",) + SEQ, None), P("dp", None))
    out_specs = (P("dp", None), P(SEQ, "dp", None))
    return jax.shard_map(
        body, mesh=split_mesh(mesh), in_specs=in_specs, out_specs=out_specs, check_vma=False
    )
```

```python
import functools

import jax
import jax.numpy as jnp
from jax import lax
from jax.experimental import pallas as pl
from jax.experimental.pallas import tpu as pltpu
from jax.sharding import Mesh, PartitionSpec as P

DOCS = 3
NZ, NY, NC = 8, 4, 2
TOK = 128
BLOCKS = NY * NC
CHUNK = TOK * BLOCKS
TILE = 512
WIDE = TILE // 2
LANES = 128
MEMBERS = NZ * BLOCKS
PARTS = 2 * BLOCKS
CUT = 7
SEQ = ("z", "y", "core")
F32, BF16 = jnp.float32, jnp.bfloat16
MIB = 1 << 20
STEPS = (0, -1, 1, -2, 2, -3, 3, 4)
VMEM = pl.BlockSpec(memory_space=pltpu.VMEM)
SMEM = pl.BlockSpec(memory_space=pltpu.SMEM)
ANY = pl.BlockSpec(memory_space=pl.ANY)


def in_hbm(x):
    return pltpu.with_memory_space_constraint(x, pltpu.HBM)


def ring(n, k):
    return [(i, (i + k) % n) for i in range(n)]


def split_mesh(mesh):
    dp = mesh.devices.shape[0]
    return Mesh(mesh.devices.reshape(dp, NZ, NY, NC), ("dp",) + SEQ)


def params(mib):
    return pltpu.CompilerParams(vmem_limit_bytes=mib * MIB)


def cost(flops, moved):
    return pl.CostEstimate(flops=flops, bytes_accessed=moved, transcendentals=0)


def open_acts_kernel(acts_ref, units_in, out_ref, z_ref, doc_ref, buf, units_ref, sem, units_sem):
    fetch = pltpu.make_async_copy(units_in, units_ref, units_sem)
    fetch.start()
    copies = [
        pltpu.make_async_copy(acts_ref.at[:, pl.ds(i * TILE, TILE)], buf.at[i], sem.at[i])
        for i in range(NZ)
    ]
    for copy in copies:
        copy.start()
    fetch.wait()
    z, y, core = (lax.axis_index(a) for a in SEQ)
    first_end = units_ref[0, 0]
    second_end = first_end + units_ref[0, 1]
    for s, step in enumerate(STEPS):
        there = lax.rem(z + (step + NZ), NZ)
        z_ref[s] = there
        for b in range(BLOCKS):
            unit = there * BLOCKS + lax.rem(y + (NY - b // NC), NY) * NC + (core if b % NC == 0 else 1 - core)
            doc_ref[s * BLOCKS + b] = (unit >= first_end).astype(jnp.int32) + (
                unit >= second_end
            ).astype(jnp.int32)
    for i in range(NZ):
        copies[i].wait()
        out_ref[i] = buf[i].T


def open_acts(acts, units):
    return pl.pallas_call(
        open_acts_kernel,
        in_specs=[ANY, ANY],
        out_specs=[VMEM, SMEM, SMEM],
        out_shape=[
            jax.ShapeDtypeStruct((NZ, TILE, TOK), BF16),
            jax.ShapeDtypeStruct((NZ,), jnp.int32),
            jax.ShapeDtypeStruct((MEMBERS,), jnp.int32),
        ],
        scratch_shapes=[
            pltpu.VMEM((NZ, TOK, TILE), BF16),
            pltpu.SMEM((1, DOCS), jnp.int32),
            pltpu.SemaphoreType.DMA((NZ,)),
            pltpu.SemaphoreType.DMA,
        ],
        compiler_params=params(8),
        cost_estimate=cost(0, 2 * MIB),
        name="open_acts",
    )(in_hbm(acts), in_hbm(units))


def open_grads_kernel(grads_ref, kept_ref, given_ref, sem):
    y, core = lax.axis_index("y"), lax.axis_index("core")
    copies = []
    for j, (out, c) in enumerate(((given_ref, 1 - core), (kept_ref, core))):
        for k in range(NY):
            tile = lax.rem(y + k, NY) * NC + c
            for h in range(2):
                cols = pl.ds(pl.multiple_of(tile * TILE + h * WIDE, WIDE), WIDE)
                copies.append(
                    pltpu.make_async_copy(grads_ref.at[:, cols], out.at[k, h], sem.at[j, k, h])
                )
    for copy in copies:
        copy.start()
    for copy in copies:
        copy.wait()


def open_grads(grads):
    shape = jax.ShapeDtypeStruct((NY, 2, TOK, WIDE), BF16)
    return pl.pallas_call(
        open_grads_kernel,
        in_specs=[ANY],
        out_specs=[VMEM] * 2,
        out_shape=[shape] * 2,
        scratch_shapes=[pltpu.SemaphoreType.DMA((NC, NY, 2))],
        compiler_params=params(4),
        cost_estimate=cost(0, 2 * MIB),
        name="open_grads",
    )(in_hbm(grads))


def pair_kernel(kept_ref, got_ref, *outs):
    for k in range(NY):
        for h in range(2):
            outs[k][h, 0] = kept_ref[k, h]
            outs[k][h, 1] = got_ref[k, h]


def pair_up(kept, got):
    return pl.pallas_call(
        pair_kernel,
        in_specs=[VMEM] * 2,
        out_specs=[VMEM] * NY,
        out_shape=[jax.ShapeDtypeStruct((2, NC, TOK, WIDE), BF16)] * NY,
        compiler_params=params(8),
        cost_estimate=cost(0, 2 * MIB),
        name="pair_up",
    )(kept, got)


def join_kernel(*refs):
    for h in range(2):
        for k in range(NY):
            refs[NY][pl.ds(h * BLOCKS + k * NC, NC)] = refs[k][h]


def join(pairs):
    return pl.pallas_call(
        join_kernel,
        in_specs=[VMEM] * NY,
        out_specs=VMEM,
        out_shape=jax.ShapeDtypeStruct((PARTS, TOK, WIDE), BF16),
        compiler_params=params(8),
        cost_estimate=cost(0, 2 * MIB),
        name="join",
    )(*pairs)


PIECES = (
    (0, 0, TILE),
    (1, 0, TILE),
    (2, 0, TILE),
    (3, 0, TILE),
    (4, 0, WIDE),
    (4, WIDE, WIDE),
    (5, 0, WIDE),
    (5, WIDE, WIDE),
    (6, 0, TILE),
    (7, 0, TILE),
)
ACTS = len(PIECES)


def acts_copies(acts, z, buf, sem):
    return [
        pltpu.make_async_copy(ref.at[z], buf.at[b, pl.ds(row, rows)], sem.at[i])
        for i, (ref, (b, row, rows)) in enumerate(zip(acts, PIECES))
    ]


def part_of(parts, h, b):
    i = h * BLOCKS + b
    if len(parts) == 1:
        return parts[0][i]
    return parts[0][i] if i < CUT else parts[1][i - CUT]


def side_by_side(buf):
    return jnp.concatenate([buf[b] for b in range(BLOCKS)], axis=1)


def norm_kernel(chunks, is_last, z_ref, doc_ref, *refs):
    n = len(chunks)
    many = 2 if is_last else n
    if is_last:
        late_ref, refs = refs[0], refs[1:]
    else:
        acts, refs = refs[:ACTS], refs[ACTS:]
    grads, refs = refs[:many], refs[many:]
    acc_ref, refs = refs[0], refs[1:]
    if is_last:
        (out_ref,) = refs
    else:
        late_ref, acts_buf, grads_buf, sem = refs
    copies = []
    for i, s in enumerate(chunks):
        copies.append([])
        if not is_last:
            copies[-1] += acts_copies(acts, z_ref[s], acts_buf.at[i], sem.at[i])
            copies[-1].append(
                pltpu.make_async_copy(grads[i], grads_buf.at[i], sem.at[i, ACTS])
            )
    for several in copies:
        for copy in several:
            copy.start()
    if not is_last:
        late_copies = acts_copies(acts, z_ref[NZ - 1], late_ref, sem.at[n])
        for copy in late_copies:
            copy.start()
        acc_ref[...] = jnp.zeros_like(acc_ref)
    for i, s in enumerate(chunks):
        for copy in copies[i]:
            copy.wait()
        for d in range(DOCS):
            held = [doc_ref[s * BLOCKS + b] == d for b in range(BLOCKS)]

            @pl.when(functools.reduce(jnp.logical_or, held))
            def _():
                x = side_by_side(late_ref if is_last else acts_buf.at[i])
                for h in range(2):
                    parts = grads if is_last else (grads_buf.at[i],)
                    kept = [
                        jnp.where(held[b], part_of(parts, h, b), jnp.zeros((TOK, WIDE), BF16))
                        for b in range(BLOCKS)
                    ]
                    acc_ref[d, :, h * WIDE : (h + 1) * WIDE] += jnp.dot(
                        x, jnp.concatenate(kept, axis=0), preferred_element_type=F32
                    )

    if not is_last:
        for copy in late_copies:
            copy.wait()
    else:
        lane = lax.broadcasted_iota(jnp.int32, (1, LANES), 1)
        row = jnp.zeros((1, LANES), F32)
        for d in range(DOCS):
            total = acc_ref[d]
            row = jnp.where(lane == d, jnp.sum(total * total), row)
        out_ref[...] = jnp.broadcast_to(row[None], out_ref.shape)


def norm_call(chunks, z_list, docs, acts, grads, sums=None):
    n = len(chunks)
    is_last = sums is not None
    operands = [z_list, docs]
    if is_last:
        acc, late = sums
        operands += [late, *grads[chunks[0]], acc]
        out_shape = jax.ShapeDtypeStruct((MEMBERS, 1, LANES), F32)
        scratch = []
    else:
        operands += map(in_hbm, [*acts, *(grads[s] for s in chunks)])
        out_shape = [
            jax.ShapeDtypeStruct((DOCS, TILE, TILE), F32),
            jax.ShapeDtypeStruct((BLOCKS, TILE, TOK), BF16),
        ]
        scratch = [
            pltpu.VMEM((n, BLOCKS, TILE, TOK), BF16),
            pltpu.VMEM((n, PARTS, TOK, WIDE), BF16),
            pltpu.SemaphoreType.DMA((n + 1, ACTS + 2)),
        ]
    return pl.pallas_call(
        functools.partial(norm_kernel, chunks, is_last),
        in_specs=[SMEM] * 2 + [VMEM if is_last else ANY] * (len(operands) - 2),
        out_specs=VMEM if is_last else [VMEM] * 2,
        out_shape=out_shape,
        scratch_shapes=scratch,
        compiler_params=params(12 + 2 * n),
        cost_estimate=cost(2 * n * CHUNK * TILE * TILE, 3 * n * MIB),
        name="norm_" + "_".join(str(s) for s in chunks),
    )(*operands)


SHARES = ((0, 0, TOK), (2, 0, TOK // 2), (2, TOK // 2, TOK // 2), (1, 0, TOK), (3, 0, TOK))


def grad_kernel(z_ref, doc_ref, norm_ref, *refs):
    acts, refs = refs[:ACTS], refs[ACTS:]
    grads, refs = refs[: NZ - 1], refs[NZ - 1 :]
    late_acts, late_grads, refs = refs[0], refs[1:3], refs[3:]
    outs, ratio_ref, acc_ref, acts_buf, grads_buf, sem = refs[:5], *refs[5:]
    copies = []
    for s in range(NZ - 1):
        copies.append(
            [pltpu.make_async_copy(grads[s], grads_buf.at[s], sem.at[s, ACTS])]
            + acts_copies(acts, z_ref[s], acts_buf.at[s], sem.at[s])
        )
        for copy in copies[s]:
            copy.start()
    squares = jnp.sum(norm_ref[...], axis=0)
    doc_norm = jnp.where(squares > 0, jnp.sqrt(squares), 0)
    lane = lax.broadcasted_iota(jnp.int32, (1, LANES), 1)
    threshold = jnp.sum(doc_norm, axis=1, keepdims=True) / DOCS
    ratio_ref[...] = doc_norm / threshold
    factor = 1.0 / jnp.maximum(doc_norm, threshold)
    clip = [jnp.sum(jnp.where(lane == d, factor, 0)) for d in range(DOCS)]
    for s in (NZ - 1, *range(NZ - 1)):
        if s < NZ - 1:
            for copy in copies[s]:
                copy.wait()
        parts = (grads_buf.at[s],) if s < NZ - 1 else late_grads
        x = side_by_side(acts_buf.at[s] if s < NZ - 1 else late_acts)
        for h in range(2):
            scaled = []
            for b in range(BLOCKS):
                doc = doc_ref[s * BLOCKS + b]
                mine = jnp.where(doc == 0, clip[0], jnp.where(doc == 1, clip[1], clip[2]))
                scaled.append((mine * part_of(parts, h, b).astype(F32)).astype(BF16))
            product = jnp.dot(
                x,
                jnp.concatenate(scaled, axis=0),
                preferred_element_type=F32,
            )
            cols = slice(h * WIDE, (h + 1) * WIDE)
            if s == NZ - 1:
                acc_ref[:, cols] = product
            else:
                acc_ref[:, cols] += product
    me = lax.axis_index("dp")
    for out, (k, row, rows) in zip(outs, SHARES):
        first = pl.multiple_of(lax.rem(me + k, 4) * TOK + row, rows)
        out[...] = acc_ref[pl.ds(first, rows), :]


def grad_call(z_list, docs, norms, acts, grads, late):
    operands = [z_list, docs, norms, *map(in_hbm, acts)]
    operands += map(in_hbm, grads[:-1])
    operands += [late, *grads[-1]]
    return pl.pallas_call(
        grad_kernel,
        in_specs=[SMEM] * 2 + [VMEM] + [ANY] * (ACTS + NZ - 1) + [VMEM] * 3,
        out_specs=[VMEM] * 6,
        out_shape=[jax.ShapeDtypeStruct((rows, TILE), F32) for _, _, rows in SHARES]
        + [jax.ShapeDtypeStruct((1, LANES), F32)],
        scratch_shapes=[
            pltpu.VMEM((TILE, TILE), F32),
            pltpu.VMEM((NZ - 1, BLOCKS, TILE, TOK), BF16),
            pltpu.VMEM((NZ - 1, PARTS, TOK, WIDE), BF16),
            pltpu.SemaphoreType.DMA((NZ - 1, ACTS + 1)),
        ],
        compiler_params=params(32),
        cost_estimate=cost(2 * NZ * CHUNK * TILE * TILE, 18 * MIB),
        name="grad",
    )(*operands)


def body(hidden_states, q_grads, doc_units):
    def after(x, *done):
        return lax.optimization_barrier((x, *done))[0]

    def move(x, axis, k):
        return lax.ppermute(x, axis, ring(lax.axis_size(axis), k))


    kept, given = open_grads(q_grads)
    got = move(given, "core", 1)
    pair = pair_up(kept, got)
    near = {k: move(pair[k], "y", k) for k in (2, 1, 3)}
    here = join([pair[0], near[1], near[2], near[3]])

    acts_t, z_list, docs = open_acts(hidden_states, doc_units)
    own = lax.all_to_all(acts_t, "z", split_axis=0, concat_axis=0, tiled=True)

    g = {0: here}
    right, left = move(own, "y", 1), move(own, "y", -1)
    own_c = move(own, "core", 1)
    for s in (1, 2):
        g[-s], g[s] = move(g[1 - s], "z", 1), move(g[s - 1], "z", -1)
    g[-3] = move(after(g[-2], right, left), "z", 1)
    g[3] = move(after(g[2], right, left), "z", -1)
    far = [move(right[:, :WIDE], "y", 1), move(left[:, WIDE:], "y", -1)]
    right_c, left_c = move(right, "core", 1), move(left, "core", 1)
    last = [
        move(after(g[-3][:CUT], *far, right_c, left_c), "z", 1),
        move(after(g[3][CUT:], *far, right_c, left_c), "z", -1),
    ]
    acts = [own, own_c, right, right_c, *far, *(move(x, "core", 1) for x in far), left, left_c]
    chunks = [g[s] for s in STEPS[:-1]] + [last]
    sums = norm_call((0, 1, 2, 3, 4, 5, 6), z_list, docs, acts, chunks)
    partial = norm_call((7,), z_list, docs, acts, chunks, sums)
    norms = lax.all_to_all(partial, SEQ, split_axis=0, concat_axis=0, tiled=True)

    *parts, ratio = grad_call(z_list, docs, norms, acts, chunks, sums[1])
    came = [move(part, "dp", k) for part, (k, _, _) in zip(parts[1:], SHARES[1:])]
    total = parts[0] + jnp.concatenate(came[:2], axis=0) + came[2] + came[3]
    return (ratio[:, :DOCS], (total * (4096 / 12))[None])


def solution(mesh):
    in_specs = (P(("dp",) + SEQ, None), P(("dp",) + SEQ, None), P("dp", None))
    out_specs = (P("dp", None), P(SEQ, "dp", None))
    return jax.shard_map(
        body, mesh=split_mesh(mesh), in_specs=in_specs, out_specs=out_specs, check_vma=False
    )
```
